32 devices in a mesh: img: 16 (over z, y, x), lm: 2 (over core).
Axes of the slice: x: 2, y: 2, z: 4, core: 2. Of those that a mesh axis runs over, the one named last changes fastest.
Arguments:
- jac_point: float32 [6, 65536], P(None, ('img', 'lm')), may hold values from -4 to 4
- jac_cam: bfloat16 [65536, 256], P(('img', 'lm')), may hold values from -0.125 to 0.125
- resid: float32 [2, 65536], P(None, ('img', 'lm')), may hold values from -6 to 6
- point_ids: int32 [65536], P(('img', 'lm')), may hold values from 0 to 4095
- cam_ids: int32 [65536], P(('img', 'lm')), may hold values from 0 to 63
- owner_slot: int32 [64], replicated, may hold values from 0 to 63, each once
- damping: float32 [1], replicated, may hold values from 0.1 to 1
Outputs:
- landmark_step: float32 [3, 8192], P(None, 'lm')
- camera_gradient: float32 [64, 128], P(('img', 'lm'))
The draws below stay inside these ranges and needn't reach their ends.
All inputs are finite; a program needn't handle non-finite values.
Results may differ from the reference program's by a relative error of at most 0.0029.
Values sent between devices are 32-bit elements; how exact they have to be, the bound alone decides.
A program may use at most 64 MiB of HBM per device.

```python
import math
import jax
import jax.numpy as jnp
import numpy as np
from jax import lax

CAMP = 128
BLOCK = 64
OBS_DEV = 2048
LM_BLOCKS = 64
GPD = 2
LANDMARKS = 8192
GROUPS = 64
OBS = 65536
N_LM = 2


def plant(result, rng, least, top_value):
    extent = result.shape
    place = [jax.random.randint(jax.random.fold_in(rng, axis), (), 0, extent[axis]) for axis in range(len(extent))]
    result = result.at[tuple(place)].set(least)
    longest = extent.index(max(extent))
    place[longest] = (place[longest] + 1) % extent[longest]
    return result.at[tuple(place)].set(top_value)


def levels(own_key, shape, pieces, low, high):
    def one(position, shards_of):
        draws = jax.random.uniform(jax.random.fold_in(jax.random.fold_in(own_key, 6), position), (shards_of,), jnp.float32, low / len(pieces), high / len(pieces))
        return jnp.repeat(jnp.exp(draws), shape[position] // shards_of).reshape((-1,) + (1,) * (len(shape) - position - 1))

    level = one(*pieces[0])
    for cut in pieces[1:]:
        level = level * one(*cut)
    return level


def cumulative_ranks(count, skew):
    portions = [(1 << 20) // math.isqrt(grade ** skew) + 1 for grade in range(1, count + 1)]
    scale = 1 + sum(portions) // (1 << 30)
    return np.cumsum(np.array([max(1, weight // scale) for weight in portions]))


def ranked(stream_key, extent, count, skew):
    listing = cumulative_ranks(count, skew)
    ticket = jax.random.randint(jax.random.fold_in(stream_key, 1), extent, 0, int(listing[count - 1]))
    standing = jnp.searchsorted(jnp.asarray(listing, jnp.int32), ticket, side="right")
    return jax.random.permutation(jax.random.fold_in(stream_key, 2), count)[standing].astype(jnp.int32)


def normal_values(key, shape, scale, limit, shards=(), kind=jnp.bfloat16):
    level = levels(key, shape, shards, -0.22, 0.18) if shards else 1.0
    entries = jax.random.normal(key, shape, jnp.float32) * scale * level
    return jnp.minimum(jnp.maximum(entries, -limit), limit).astype(kind)


def setup_inputs(seed: int = 0) -> dict:
    keys = jax.random.split(jax.random.key(seed), 8)
    return {
        "jac_point": normal_values(keys[0], (6, OBS), 0.25, 4.0, ((1, 32),), jnp.float32),
        "jac_cam": normal_values(keys[1], (OBS, 2 * CAMP), (2 * OBS_DEV // GPD) ** -0.5, 0.125, ((0, 32),)),
        "resid": normal_values(keys[2], (2, OBS), 1.0, 6.0, ((1, 32),), jnp.float32),
        "point_ids": plant(jax.random.randint(keys[3], (OBS,), 0, LM_BLOCKS * BLOCK), jax.random.fold_in(keys[3], 1), 0, (LM_BLOCKS * BLOCK) - 1).astype(jnp.int32),
        "cam_ids": plant(ranked(keys[4], (OBS,), GROUPS, 1), jax.random.fold_in(keys[4], 3), 0, GROUPS - 1).astype(jnp.int32),
        "owner_slot": jax.random.permutation(keys[5], GROUPS).astype(jnp.int32),
        "damping": jnp.clip(jnp.exp(jax.random.uniform(keys[6], (1,), jnp.float32, math.log(0.1), math.log(1.0))), 0.1, 1.0),
    }


def obs_terms(jac_point, resid):
    u0, u1, u2 = jac_point[0], jac_point[1], jac_point[2]
    v0, v1, v2 = jac_point[3], jac_point[4], jac_point[5]
    ru, rv = resid[0], resid[1]
    return jnp.stack([u0 * u0 + v0 * v0, u0 * u1 + v0 * v1, u0 * u2 + v0 * v2,
                      u1 * u1 + v1 * v1, u1 * u2 + v1 * v2, u2 * u2 + v2 * v2,
                      u0 * ru + v0 * rv, u1 * ru + v1 * rv, u2 * ru + v2 * rv], axis=1)


def solve_points(stats, damping):
    factor = damping[0]
    h01, h02, h12 = stats[1], stats[2], stats[4]
    a00 = stats[0] + factor * (stats[0] + 1.0)
    a11 = stats[3] + factor * (stats[3] + 1.0)
    a22 = stats[5] + factor * (stats[5] + 1.0)
    g0, g1, g2 = stats[6], stats[7], stats[8]
    c00 = a11 * a22 - h12 * h12
    c01 = h02 * h12 - h01 * a22
    c02 = h01 * h12 - h02 * a11
    c11 = a00 * a22 - h02 * h02
    c12 = h01 * h02 - a00 * h12
    c22 = a00 * a11 - h01 * h01
    determ = a00 * c00 + h01 * c01 + h02 * c02
    s0 = -(c00 * g0 + c01 * g1 + c02 * g2) / determ
    s1 = -(c01 * g0 + c11 * g1 + c12 * g2) / determ
    s2 = -(c02 * g0 + c12 * g1 + c22 * g2) / determ
    return jnp.stack([s0, s1, s2], axis=0)


def correct(jac_point, resid, step_obs):
    cu = resid[0] + jac_point[0] * step_obs[0] + jac_point[1] * step_obs[1] + jac_point[2] * step_obs[2]
    cv = resid[1] + jac_point[3] * step_obs[0] + jac_point[4] * step_obs[1] + jac_point[5] * step_obs[2]
    return cu, cv


def reference(jac_point, jac_cam, resid, point_ids, cam_ids, owner_slot, damping):
    total = point_ids.shape[0]
    slice_points = LM_BLOCKS * BLOCK
    rows = jnp.arange(total, dtype=jnp.int32)
    landmark = ((rows // OBS_DEV) % N_LM) * slice_points + point_ids
    terms = obs_terms(jac_point, resid)
    stats = jax.ops.segment_sum(terms, landmark, num_segments=LANDMARKS).T
    step = solve_points(stats, damping)
    cu, cv = correct(jac_point, resid, step[:, landmark])
    cu = lax.optimization_barrier(cu.astype(jnp.bfloat16)).astype(jnp.float32)
    cv = lax.optimization_barrier(cv.astype(jnp.bfloat16)).astype(jnp.float32)
    slots = owner_slot[cam_ids]
    devices = total // OBS_DEV
    cu_b = cu.reshape(devices, OBS_DEV)
    cv_b = cv.reshape(devices, OBS_DEV)
    cam_b = jac_cam.reshape(devices, OBS_DEV, 2 * CAMP)
    slot_b = slots.reshape(devices, OBS_DEV)

    def add_block(carry, items):
        bu, bv, bcam, bslot = items
        contrib = bu[:, None] * bcam[:, :CAMP].astype(jnp.float32) + bv[:, None] * bcam[:, CAMP:].astype(jnp.float32)
        return carry + jax.ops.segment_sum(contrib, bslot, num_segments=GROUPS), None

    init = jnp.zeros((GROUPS, CAMP), jnp.float32)
    gradient, _ = lax.scan(add_block, init, (cu_b, cv_b, cam_b, slot_b))
    return step, gradient
```

```python
import functools
import jax
import jax.numpy as jnp
from jax import lax
from jax.experimental import pallas as pl
from jax.experimental.pallas import tpu as pltpu
from jax.sharding import PartitionSpec as P

CAMP = 128
BLOCK = 64
LM_BLOCKS = 64
LANES = 128
WIDE = 256
MESH = pl.DeviceIdType.MESH
F32 = jnp.float32
BF16 = jnp.bfloat16


def split_pair(x):
    high = x.astype(BF16).astype(F32)
    low = (x - high).astype(BF16).astype(F32)
    return high, low


def solve_points(stats, factor):
    h01, h02, h12 = (stats[1], stats[2], stats[4])
    a00 = stats[0] + factor * (stats[0] + 1.0)
    a11 = stats[3] + factor * (stats[3] + 1.0)
    a22 = stats[5] + factor * (stats[5] + 1.0)
    g0, g1, g2 = (stats[6], stats[7], stats[8])
    c00 = a11 * a22 - h12 * h12
    c01 = h02 * h12 - h01 * a22
    c02 = h01 * h12 - h02 * a11
    c11 = a00 * a22 - h02 * h02
    c12 = h01 * h02 - a00 * h12
    c22 = a00 * a11 - h01 * h01
    determ = a00 * c00 + h01 * c01 + h02 * c02
    s0 = -(c00 * g0 + c01 * g1 + c02 * g2) / determ
    s1 = -(c01 * g0 + c11 * g1 + c12 * g2) / determ
    s2 = -(c02 * g0 + c12 * g1 + c22 * g2) / determ
    return s0, s1, s2


def kernel(
    n_img, n_lm, n_own, groups,
    damping_ref, jac_ref, resid_ref, point_ref, cam_ref, slot_ref, jac_cam_ref,
    step_ref, grad_ref,
    cam_vmem, lo_hot, stat_send, stat_recv, table, part_send, part_recv,
    cam_sem, stat_send_sem, stat_recv_sem, extra_sem,
    step_send_sem, step_recv_sem, part_send_sem, part_recv_sem,
):
    n_dev = n_img * n_lm
    n_obs = point_ref.shape[1]
    rows = LM_BLOCKS * BLOCK // LANES
    n_hi = LM_BLOCKS * BLOCK // WIDE
    per_row = rows // n_own
    stride = n_img // n_own
    gpd = groups // n_dev
    img, lm = lax.axis_index("img"), lax.axis_index("lm")
    me = img * n_lm + lm
    own = img // stride if stride > 1 else img

    barrier = pltpu.get_barrier_semaphore()

    def greet(r, carry):
        peer = lax.rem(me + r, n_dev)
        pl.semaphore_signal(
            barrier, inc=1, device_id=(peer // n_lm, lax.rem(peer, n_lm)), device_id_type=MESH
        )
        return carry

    lax.fori_loop(1, n_dev, greet, 0)
    cam_copy = pltpu.make_async_copy(jac_cam_ref, cam_vmem, cam_sem)
    cam_copy.start()

    u = [jac_ref[a : a + 1, :] for a in range(3)]
    v = [jac_ref[3 + a : 4 + a, :] for a in range(3)]
    ru, rv = resid_ref[0:1, :], resid_ref[1:2, :]
    terms = [u[a] * u[b] + v[a] * v[b] for a, b in ((0, 0), (0, 1), (0, 2), (1, 1), (1, 2), (2, 2))]
    terms += [u[a] * ru + v[a] * rv for a in range(3)]
    point = point_ref[...]
    hi = point // WIDE
    lo = point - hi * WIDE
    hi_mask = lax.broadcasted_iota(jnp.int32, (n_hi, n_obs), 0) == hi
    lo_hot[...] = jnp.where(
        lax.broadcasted_iota(jnp.int32, (WIDE, n_obs), 0) == lo, 1.0, 0.0
    ).astype(BF16)
    blocks = []
    for part in zip(*[split_pair(t) for t in terms]):
        blocks += [jnp.where(hi_mask, t, 0.0).astype(BF16) for t in part]
    left = jnp.concatenate(blocks, axis=0)
    both = lax.dot_general(
        left, lo_hot[...], (((1,), (1,)), ((), ())), preferred_element_type=F32
    )
    local = both[: 9 * n_hi] + both[9 * n_hi :]
    for k in range(9):
        for half in range(WIDE // LANES):
            piece = local[k * n_hi : (k + 1) * n_hi, half * LANES : (half + 1) * LANES]
            if per_row == 2:
                stat_send[:, k, half, :] = piece
            else:
                for h in range(n_hi):
                    stat_send[h * (WIDE // LANES) + half, k] = piece[h : h + 1]

    pl.semaphore_wait(barrier, n_dev - 1)

    def send_stats(r, sem):
        owner = lax.rem(own + r, n_own)
        target = owner * stride
        return pltpu.make_async_remote_copy(
            src_ref=stat_send.at[owner],
            dst_ref=stat_recv.at[lax.rem(img - target + n_img - 1, n_img)],
            send_sem=sem,
            recv_sem=stat_recv_sem,
            device_id=(target, lm),
            device_id_type=MESH,
        )

    def stats_step(r, carry):
        send_stats(r, stat_send_sem).start()
        return carry

    lax.fori_loop(1, n_own, stats_step, 0)

    def step_copy(r):
        block = table.at[pl.ds(own * per_row, per_row)]
        return pltpu.make_async_remote_copy(
            src_ref=block,
            dst_ref=block,
            send_sem=step_send_sem,
            recv_sem=step_recv_sem,
            device_id=(lax.rem(img + r, n_img), lm),
            device_id_type=MESH,
        )

    def wait_for(ref, sem):
        pltpu.make_async_copy(ref, ref, sem).wait()

    def own_part():
        wait_for(stat_recv, stat_recv_sem)
        total = stat_send[own] + jnp.sum(stat_recv[...], axis=0)
        steps = solve_points([total[k] for k in range(9)], damping_ref[0])
        for half in range(per_row):
            for a in range(3):
                table[own * per_row + half, a : a + 1] = steps[a][half : half + 1]
            table[own * per_row + half, 3:4] = jnp.zeros((1, LANES), F32)

        def steps_out(r, carry):
            step_copy(r).start()
            return carry

        lax.fori_loop(1, n_img, steps_out, 0)

    row_slot = slot_ref[...]
    eye = lax.broadcasted_iota(jnp.int32, (groups, groups), 0) == lax.broadcasted_iota(
        jnp.int32, (groups, groups), 1
    )
    slot_column = jnp.sum(
        jnp.where(eye, row_slot.astype(F32), 0.0), axis=1, keepdims=True
    )
    group_iota = lax.broadcasted_iota(jnp.int32, (groups, n_obs), 0)
    slots = jnp.sum(
        jnp.where(group_iota == cam_ref[...], slot_column, 0.0), axis=0, keepdims=True
    ).astype(jnp.int32)

    if stride == 1:
        own_part()
        wait_for(table.at[pl.ds(0, rows - per_row)], step_recv_sem)
    else:
        is_owner = lax.rem(img, stride) == 0

        @pl.when(is_owner)
        def _():
            own_part()
            wait_for(table.at[pl.ds(0, rows - per_row)], step_recv_sem)

        @pl.when(jnp.logical_not(is_owner))
        def _():
            send_stats(0, extra_sem).start()
            wait_for(table, step_recv_sem)

    grid = table[...].reshape(n_hi, WIDE // LANES, 4, LANES)
    picked = [
        jnp.concatenate([grid[:, half, a, :] for half in range(WIDE // LANES)], axis=1)
        for a in range(3)
    ]
    pieces = []
    for part in zip(*[split_pair(t) for t in picked]):
        pieces += [t.astype(BF16) for t in part]
    found = jnp.dot(jnp.concatenate(pieces, axis=0), lo_hot[...], preferred_element_type=F32)
    step_obs = []
    for a in range(3):
        both_parts = found[a * n_hi : (a + 1) * n_hi] + found[(3 + a) * n_hi : (4 + a) * n_hi]
        step_obs.append(jnp.sum(jnp.where(hi_mask, both_parts, 0.0), axis=0, keepdims=True))
    cu = ru + u[0] * step_obs[0] + u[1] * step_obs[1] + u[2] * step_obs[2]
    cv = rv + v[0] * step_obs[0] + v[1] * step_obs[1] + v[2] * step_obs[2]
    member = group_iota == slots
    weights = jnp.concatenate(
        [jnp.where(member, cu, 0.0).astype(BF16), jnp.where(member, cv, 0.0).astype(BF16)], axis=0
    )
    cam_copy.wait()
    product = jnp.dot(weights, cam_vmem[...], preferred_element_type=F32)
    partial = product[:groups, :CAMP] + product[groups:, CAMP:]
    part_send[...] = partial.reshape(n_dev, gpd, CAMP)

    def part_step(r, carry):
        peer = lax.rem(me + r, n_dev)
        pltpu.make_async_remote_copy(
            src_ref=part_send.at[peer],
            dst_ref=part_recv.at[r - 1],
            send_sem=part_send_sem,
            recv_sem=part_recv_sem,
            device_id=(peer // n_lm, lax.rem(peer, n_lm)),
            device_id_type=MESH,
        ).start()
        return carry

    lax.fori_loop(1, n_dev, part_step, 0)

    for row in range(rows):
        step_ref[:, row * LANES : (row + 1) * LANES] = table[row, 0:3]

    wait_for(stat_send.at[pl.ds(0, n_own - 1)], stat_send_sem)
    if stride == 1:
        wait_for(table.at[pl.ds(0, rows - per_row)], step_send_sem)
    else:

        @pl.when(is_owner)
        def _():
            def one_step(r, carry):
                wait_for(table.at[pl.ds(0, per_row)], step_send_sem)
                return carry

            lax.fori_loop(1, n_img, one_step, 0)

        @pl.when(jnp.logical_not(is_owner))
        def _():
            wait_for(stat_send.at[0], extra_sem)

    wait_for(part_recv, part_recv_sem)
    grad_ref[...] = part_send[me] + jnp.sum(part_recv[...], axis=0)
    wait_for(part_send.at[pl.ds(0, n_dev - 1)], part_send_sem)


def solution(mesh):
    n_img, n_lm = mesh.shape["img"], mesh.shape["lm"]
    n_dev = n_img * n_lm
    points = LM_BLOCKS * BLOCK
    rows = points // LANES
    n_own = min(n_img, rows)
    per_row = rows // n_own

    def per_device(jac_point, jac_cam, resid, point_ids, cam_ids, owner_slot, damping):
        n_obs = cam_ids.shape[0]
        groups = owner_slot.shape[0]
        gpd = groups // n_dev
        vmem = pl.BlockSpec(memory_space=pltpu.VMEM)
        return pl.pallas_call(
            functools.partial(kernel, n_img, n_lm, n_own, groups),
            out_shape=(
                jax.ShapeDtypeStruct((3, points), F32),
                jax.ShapeDtypeStruct((gpd, CAMP), F32),
            ),
            in_specs=[pl.BlockSpec(memory_space=pltpu.SMEM)]
            + [vmem] * 5
            + [pl.BlockSpec(memory_space=pl.ANY)],
            out_specs=(vmem, vmem),
            scratch_shapes=[
                pltpu.VMEM((n_obs, 2 * CAMP), BF16),
                pltpu.VMEM((WIDE, n_obs), BF16),
                pltpu.VMEM((n_own, 9, per_row, LANES), F32),
                pltpu.VMEM((n_img - 1, 9, per_row, LANES), F32),
                pltpu.VMEM((rows, 4, LANES), F32),
                pltpu.VMEM((n_dev, gpd, CAMP), F32),
                pltpu.VMEM((n_dev - 1, gpd, CAMP), F32),
            ]
            + [pltpu.SemaphoreType.DMA] * 8,
            compiler_params=pltpu.CompilerParams(
                collective_id=0,
                has_side_effects=True,
                vmem_limit_bytes=(24 if groups <= 256 else 56) * 2**20,
            ),
        )(
            damping,
            jac_point,
            resid,
            point_ids.reshape(1, n_obs),
            cam_ids.reshape(1, n_obs),
            owner_slot.reshape(1, groups),
            jac_cam,
        )

    placed = (
        P(None, ("img", "lm")),
        P(("img", "lm"), None),
        P(None, ("img", "lm")),
        P(("img", "lm")),
        P(("img", "lm")),
        P(),
        P(),
    )
    return jax.shard_map(
        per_device,
        mesh=mesh,
        in_specs=placed,
        out_specs=(P(None, "lm"), P(("img", "lm"), None)),
        check_vma=False,
    )
```

```python
import functools
import jax
import jax.numpy as jnp
from jax import lax
from jax.experimental import pallas as pl
from jax.experimental.pallas import tpu as pltpu
from jax.sharding import PartitionSpec as P

CAMP = 128
BLOCK = 64
LM_BLOCKS = 64
LANES = 128
VMEM_BYTES = 2**26 - 2**18
WIDE = 256
MESH = pl.DeviceIdType.MESH
F32 = jnp.float32
BF16 = jnp.bfloat16


def split_pair(x):
    high = x.astype(BF16).astype(F32)
    low = (x - high).astype(BF16).astype(F32)
    return high, low


def solve_points(stats, factor):
    h01, h02, h12 = (stats[1], stats[2], stats[4])
    a00 = stats[0] + factor * (stats[0] + 1.0)
    a11 = stats[3] + factor * (stats[3] + 1.0)
    a22 = stats[5] + factor * (stats[5] + 1.0)
    g0, g1, g2 = (stats[6], stats[7], stats[8])
    c00 = a11 * a22 - h12 * h12
    c01 = h02 * h12 - h01 * a22
    c02 = h01 * h12 - h02 * a11
    c11 = a00 * a22 - h02 * h02
    c12 = h01 * h02 - a00 * h12
    c22 = a00 * a11 - h01 * h01
    determ = a00 * c00 + h01 * c01 + h02 * c02
    s0 = -(c00 * g0 + c01 * g1 + c02 * g2) / determ
    s1 = -(c01 * g0 + c11 * g1 + c12 * g2) / determ
    s2 = -(c02 * g0 + c12 * g1 + c22 * g2) / determ
    return s0, s1, s2


def kernel(
    n_img, n_lm, n_own, groups,
    damping_ref, jac_hbm, resid_hbm, point_hbm, cam_hbm, slot_hbm, jac_cam_hbm,
    step_hbm, grad_hbm,
    step_ref, grad_ref, jac_ref, resid_ref, point_ref, cam_ref, slot_ref, cam_vmem, lo_hot, stat_send, stat_recv, table, part_send, part_recv,
    in_sems, out_sems, stat_send_sem, stat_recv_sem, extra_sem,
    step_send_sem, step_recv_sem, part_send_sem, part_recv_sem,
):
    n_dev = n_img * n_lm
    n_obs = point_ref.shape[1]
    rows = LM_BLOCKS * BLOCK // LANES
    n_hi = LM_BLOCKS * BLOCK // WIDE
    per_row = rows // n_own
    stride = n_img // n_own
    gpd = groups // n_dev
    img, lm = lax.axis_index("img"), lax.axis_index("lm")
    me = img * n_lm + lm
    own = img // stride if stride > 1 else img

    copies = [
        pltpu.make_async_copy(source, target, in_sems.at[i])
        for i, (source, target) in enumerate(
            [
                (point_hbm, point_ref),
                (jac_hbm, jac_ref),
                (resid_hbm, resid_ref),
                (cam_hbm, cam_ref),
                (slot_hbm, slot_ref),
                (jac_cam_hbm, cam_vmem),
            ]
        )
    ]
    for copy in copies:
        copy.start()

    def wrap(index, extent):
        return jnp.where(index >= extent, index - extent, index)

    def repeat(first, last, body):
        if last <= 64:
            for r in range(first, last):
                body(r)
        else:
            lax.fori_loop(first, last, lambda r, carry: (body(r), carry)[1], 0)

    def every_peer(body):
        for d_lm in range(n_lm):
            peer_lm = wrap(lm + d_lm, n_lm)

            def one(d_img, d_lm=d_lm, peer_lm=peer_lm):
                body(wrap(img + d_img, n_img), peer_lm, d_img * n_lm + d_lm - 1)

            repeat(1 if d_lm == 0 else 0, n_img, one)

    barrier = pltpu.get_barrier_semaphore()
    every_peer(
        lambda peer_img, peer_lm, r: pl.semaphore_signal(
            barrier, inc=1, device_id=(peer_img, peer_lm), device_id_type=MESH
        )
    )

    copies[0].wait()
    point = point_ref[...]
    hi = point // WIDE
    lo = point - hi * WIDE
    hi_mask = lax.broadcasted_iota(jnp.int32, (n_hi, n_obs), 0) == hi
    lo_hot[...] = jnp.where(
        lax.broadcasted_iota(jnp.int32, (WIDE, n_obs), 0) == lo, 1.0, 0.0
    ).astype(BF16)
    copies[1].wait()
    copies[2].wait()
    u = [jac_ref[a : a + 1, :] for a in range(3)]
    v = [jac_ref[3 + a : 4 + a, :] for a in range(3)]
    ru, rv = resid_ref[0:1, :], resid_ref[1:2, :]
    terms = [u[a] * u[b] + v[a] * v[b] for a, b in ((0, 0), (0, 1), (0, 2), (1, 1), (1, 2), (2, 2))]
    terms += [u[a] * ru + v[a] * rv for a in range(3)]
    blocks = []
    for part in zip(*[split_pair(t) for t in terms]):
        blocks += [jnp.where(hi_mask, t, 0.0).astype(BF16) for t in part]
    left = jnp.concatenate(blocks, axis=0)
    both = lax.dot_general(
        left, lo_hot[...], (((1,), (1,)), ((), ())), preferred_element_type=F32
    )
    local = both[: 9 * n_hi] + both[9 * n_hi :]
    for k in range(9):
        for half in range(WIDE // LANES):
            piece = local[k * n_hi : (k + 1) * n_hi, half * LANES : (half + 1) * LANES]
            if per_row == 2:
                stat_send[:, k, half, :] = piece
            else:
                for h in range(n_hi):
                    stat_send[h * (WIDE // LANES) + half, k] = piece[h : h + 1]

    pl.semaphore_wait(barrier, n_dev - 1)

    def send_stats(r, sem):
        owner = wrap(own + r, n_own)
        target = owner * stride
        return pltpu.make_async_remote_copy(
            src_ref=stat_send.at[owner],
            dst_ref=stat_recv.at[wrap(img - target + n_img - 1, n_img)],
            send_sem=sem,
            recv_sem=stat_recv_sem,
            device_id=(target, lm),
            device_id_type=MESH,
        )

    repeat(1, n_own, lambda r: send_stats(r, stat_send_sem).start())

    def step_copy(r):
        block = table.at[pl.ds(own * per_row, per_row)]
        return pltpu.make_async_remote_copy(
            src_ref=block,
            dst_ref=block,
            send_sem=step_send_sem,
            recv_sem=step_recv_sem,
            device_id=(wrap(img + r, n_img), lm),
            device_id_type=MESH,
        )

    def wait_for(ref, sem):
        pltpu.make_async_copy(ref, ref, sem).wait()

    def own_part():
        wait_for(stat_recv, stat_recv_sem)
        total = stat_send[own] + jnp.sum(stat_recv[...], axis=0)
        steps = solve_points([total[k] for k in range(9)], damping_ref[0])
        for half in range(per_row):
            for a in range(3):
                table[own * per_row + half, a : a + 1] = steps[a][half : half + 1]
            table[own * per_row + half, 3:4] = jnp.zeros((1, LANES), F32)
        repeat(1, n_img, lambda r: step_copy(r).start())

    copies[3].wait()
    copies[4].wait()
    row_slot = slot_ref[...]
    eye = lax.broadcasted_iota(jnp.int32, (groups, groups), 0) == lax.broadcasted_iota(
        jnp.int32, (groups, groups), 1
    )
    slot_column = jnp.sum(
        jnp.where(eye, row_slot.astype(F32), 0.0), axis=1, keepdims=True
    )
    group_iota = lax.broadcasted_iota(jnp.int32, (groups, n_obs), 0)
    slots = jnp.sum(
        jnp.where(group_iota == cam_ref[...], slot_column, 0.0), axis=0, keepdims=True
    ).astype(jnp.int32)

    if stride == 1:
        own_part()
        wait_for(table.at[pl.ds(0, rows - per_row)], step_recv_sem)
    else:
        is_owner = lax.rem(img, stride) == 0

        @pl.when(is_owner)
        def _():
            own_part()
            wait_for(table.at[pl.ds(0, rows - per_row)], step_recv_sem)

        @pl.when(jnp.logical_not(is_owner))
        def _():
            send_stats(0, extra_sem).start()
            wait_for(table, step_recv_sem)

    grid = table[...].reshape(n_hi, WIDE // LANES, 4, LANES)
    picked = [
        jnp.concatenate([grid[:, half, a, :] for half in range(WIDE // LANES)], axis=1)
        for a in range(3)
    ]
    pieces = []
    for part in zip(*[split_pair(t) for t in picked]):
        pieces += [t.astype(BF16) for t in part]
    found = jnp.dot(jnp.concatenate(pieces, axis=0), lo_hot[...], preferred_element_type=F32)
    step_obs = []
    for a in range(3):
        both_parts = found[a * n_hi : (a + 1) * n_hi] + found[(3 + a) * n_hi : (4 + a) * n_hi]
        step_obs.append(jnp.sum(jnp.where(hi_mask, both_parts, 0.0), axis=0, keepdims=True))
    cu = ru + u[0] * step_obs[0] + u[1] * step_obs[1] + u[2] * step_obs[2]
    cv = rv + v[0] * step_obs[0] + v[1] * step_obs[1] + v[2] * step_obs[2]
    member = group_iota == slots
    weights = jnp.concatenate(
        [jnp.where(member, cu, 0.0).astype(BF16), jnp.where(member, cv, 0.0).astype(BF16)], axis=0
    )
    copies[5].wait()
    product = jnp.dot(weights, cam_vmem[...], preferred_element_type=F32)
    partial = product[:groups, :CAMP] + product[groups:, CAMP:]
    part_send[...] = partial.reshape(n_dev, gpd, CAMP)

    every_peer(
        lambda peer_img, peer_lm, r: pltpu.make_async_remote_copy(
            src_ref=part_send.at[peer_img * n_lm + peer_lm],
            dst_ref=part_recv.at[r],
            send_sem=part_send_sem,
            recv_sem=part_recv_sem,
            device_id=(peer_img, peer_lm),
            device_id_type=MESH,
        ).start()
    )

    for row in range(rows):
        step_ref[:, row * LANES : (row + 1) * LANES] = table[row, 0:3]
    step_out = pltpu.make_async_copy(step_ref, step_hbm, out_sems.at[0])
    step_out.start()

    wait_for(stat_send.at[pl.ds(0, n_own - 1)], stat_send_sem)
    if stride == 1:
        wait_for(table.at[pl.ds(0, rows - per_row)], step_send_sem)
    else:

        @pl.when(is_owner)
        def _():
            def one_step(r, carry):
                wait_for(table.at[pl.ds(0, per_row)], step_send_sem)
                return carry

            lax.fori_loop(1, n_img, one_step, 0)

        @pl.when(jnp.logical_not(is_owner))
        def _():
            wait_for(stat_send.at[0], extra_sem)

    wait_for(part_recv, part_recv_sem)
    grad_ref[...] = part_send[me] + jnp.sum(part_recv[...], axis=0)
    grad_out = pltpu.make_async_copy(grad_ref, grad_hbm, out_sems.at[1])
    grad_out.start()
    wait_for(part_send.at[pl.ds(0, n_dev - 1)], part_send_sem)
    step_out.wait()
    grad_out.wait()


def write_out(step_in, grad_in, step_hbm, grad_hbm, sems):
    copies = [
        pltpu.make_async_copy(step_in, step_hbm, sems.at[0]),
        pltpu.make_async_copy(grad_in, grad_hbm, sems.at[1]),
    ]
    for copy in copies:
        copy.start()
    for copy in copies:
        copy.wait()


def solution(mesh):
    n_img, n_lm = mesh.shape["img"], mesh.shape["lm"]
    n_dev = n_img * n_lm
    points = LM_BLOCKS * BLOCK
    rows = points // LANES
    n_own = min(n_img, rows)
    per_row = rows // n_own

    def per_device(jac_point, jac_cam, resid, point_ids, cam_ids, owner_slot, damping):
        n_obs = cam_ids.shape[0]
        groups = owner_slot.shape[0]
        gpd = groups // n_dev
        hbm = pl.BlockSpec(memory_space=pltpu.HBM)
        shapes = (
            jax.ShapeDtypeStruct((3, points), F32),
            jax.ShapeDtypeStruct((gpd, CAMP), F32),
        )
        results = pl.pallas_call(
            functools.partial(kernel, n_img, n_lm, n_own, groups),
            out_shape=shapes,
            in_specs=[pl.BlockSpec(memory_space=pltpu.SMEM)]
            + [hbm] * 6,
            out_specs=(hbm, hbm),
            scratch_shapes=[
                pltpu.VMEM((3, points), F32),
                pltpu.VMEM((gpd, CAMP), F32),
                pltpu.VMEM(jac_point.shape, F32),
                pltpu.VMEM(resid.shape, F32),
                pltpu.VMEM((1, n_obs), jnp.int32),
                pltpu.VMEM((1, n_obs), jnp.int32),
                pltpu.VMEM((1, groups), jnp.int32),
                pltpu.VMEM((n_obs, 2 * CAMP), BF16),
                pltpu.VMEM((WIDE, n_obs), BF16),
                pltpu.VMEM((n_own, 9, per_row, LANES), F32),
                pltpu.VMEM((n_img - 1, 9, per_row, LANES), F32),
                pltpu.VMEM((rows, 4, LANES), F32),
                pltpu.VMEM((n_dev, gpd, CAMP), F32),
                pltpu.VMEM((n_dev - 1, gpd, CAMP), F32),
            ]
            + [pltpu.SemaphoreType.DMA((6,)), pltpu.SemaphoreType.DMA((2,))]
            + [pltpu.SemaphoreType.DMA] * 7,
            compiler_params=pltpu.CompilerParams(
                collective_id=0,
                has_side_effects=True,
                vmem_limit_bytes=VMEM_BYTES,
            ),
        )(
            damping,
            jac_point,
            resid,
            point_ids.reshape(1, n_obs),
            cam_ids.reshape(1, n_obs),
            owner_slot.reshape(1, groups),
            jac_cam,
        )
        return pl.pallas_call(
            write_out,
            out_shape=shapes,
            in_specs=[hbm, hbm],
            out_specs=(hbm, hbm),
            scratch_shapes=[pltpu.SemaphoreType.DMA((2,))],
            compiler_params=pltpu.CompilerParams(vmem_limit_bytes=VMEM_BYTES),
        )(*results)

    placed = (
        P(None, ("img", "lm")),
        P(("img", "lm"), None),
        P(None, ("img", "lm")),
        P(("img", "lm")),
        P(("img", "lm")),
        P(),
        P(),
    )
    return jax.shard_map(
        per_device,
        mesh=mesh,
        in_specs=placed,
        out_specs=(P(None, "lm"), P(("img", "lm"), None)),
        check_vma=False,
    )
```

```python
import functools
import jax
import jax.numpy as jnp
from jax import lax
from jax.experimental import pallas as pl
from jax.experimental.pallas import tpu as pltpu
from jax.sharding import PartitionSpec as P

CAMP = 128
BLOCK = 64
LM_BLOCKS = 64
LANES = 128
VMEM_BYTES = 2**26 - 2**18
WIDE = 256
CHUNK = 512
MESH = pl.DeviceIdType.MESH
F32 = jnp.float32
BF16 = jnp.bfloat16


def split_pair(x):
    high = x.astype(BF16).astype(F32)
    low = (x - high).astype(BF16).astype(F32)
    return high, low


def solve_points(stats, factor):
    h01, h02, h12 = (stats[1], stats[2], stats[4])
    a00 = stats[0] + factor * (stats[0] + 1.0)
    a11 = stats[3] + factor * (stats[3] + 1.0)
    a22 = stats[5] + factor * (stats[5] + 1.0)
    g0, g1, g2 = (stats[6], stats[7], stats[8])
    c00 = a11 * a22 - h12 * h12
    c01 = h02 * h12 - h01 * a22
    c02 = h01 * h12 - h02 * a11
    c11 = a00 * a22 - h02 * h02
    c12 = h01 * h02 - a00 * h12
    c22 = a00 * a11 - h01 * h01
    determ = a00 * c00 + h01 * c01 + h02 * c02
    s0 = -(c00 * g0 + c01 * g1 + c02 * g2) / determ
    s1 = -(c01 * g0 + c11 * g1 + c12 * g2) / determ
    s2 = -(c02 * g0 + c12 * g1 + c22 * g2) / determ
    return s0, s1, s2


def kernel(
    n_img, n_lm, n_own, groups,
    damping_ref, jac_hbm, resid_hbm, point_hbm, cam_hbm, slot_hbm, jac_cam_hbm,
    step_hbm, grad_hbm,
    step_ref, grad_ref, jac_ref, resid_ref, point_ref, cam_ref, slot_ref, slot_row, cam_vmem, lo_hot, stat_send, stat_recv, table, part_send, part_recv,
    in_sems, out_sems, stat_send_sem, stat_recv_sem, extra_sem,
    step_send_sem, step_recv_sem, part_send_sem, part_recv_sem,
):
    n_dev = n_img * n_lm
    n_obs = point_ref.shape[1]
    rows = LM_BLOCKS * BLOCK // LANES
    n_hi = LM_BLOCKS * BLOCK // WIDE
    per_row = rows // n_own
    stride = n_img // n_own
    gpd = groups // n_dev
    img, lm = lax.axis_index("img"), lax.axis_index("lm")
    me = img * n_lm + lm
    own = img // stride if stride > 1 else img

    copies = [
        pltpu.make_async_copy(source, target, in_sems.at[i])
        for i, (source, target) in enumerate(
            [
                (point_hbm, point_ref),
                (jac_hbm, jac_ref),
                (resid_hbm, resid_ref),
                (cam_hbm, cam_ref),
                (slot_hbm, slot_ref),
                (jac_cam_hbm, cam_vmem),
            ]
        )
    ]
    for copy in copies:
        copy.start()

    def wrap(index, extent):
        return jnp.where(index >= extent, index - extent, index)

    def repeat(first, last, body):
        if last <= 64:
            for r in range(first, last):
                body(r)
        else:
            lax.fori_loop(first, last, lambda r, carry: (body(r), carry)[1], 0)

    def every_peer(body):
        for d_lm in range(n_lm):
            peer_lm = wrap(lm + d_lm, n_lm)

            def one(d_img, d_lm=d_lm, peer_lm=peer_lm):
                body(wrap(img + d_img, n_img), peer_lm, d_img * n_lm + d_lm - 1)

            repeat(1 if d_lm == 0 else 0, n_img, one)

    barrier = pltpu.get_barrier_semaphore()
    every_peer(
        lambda peer_img, peer_lm, r: pl.semaphore_signal(
            barrier, inc=1, device_id=(peer_img, peer_lm), device_id_type=MESH
        )
    )

    for copy in copies[:3]:
        copy.wait()
    local = jnp.zeros((9 * n_hi, WIDE), F32)
    parts = [pl.ds(start, CHUNK) for start in range(0, n_obs, CHUNK)]
    for part in parts:
        point = point_ref[:, part]
        hi = point // WIDE
        hi_mask = lax.broadcasted_iota(jnp.int32, (n_hi, CHUNK), 0) == hi
        hot = jnp.where(
            lax.broadcasted_iota(jnp.int32, (WIDE, CHUNK), 0) == point - hi * WIDE, 1.0, 0.0
        ).astype(BF16)
        lo_hot[:, part] = hot
        u = [jac_ref[a : a + 1, part] for a in range(3)]
        v = [jac_ref[3 + a : 4 + a, part] for a in range(3)]
        ru, rv = resid_ref[0:1, part], resid_ref[1:2, part]
        pairs = ((0, 0), (0, 1), (0, 2), (1, 1), (1, 2), (2, 2))
        terms = [u[a] * u[b] + v[a] * v[b] for a, b in pairs]
        terms += [u[a] * ru + v[a] * rv for a in range(3)]
        blocks = []
        for values in zip(*[split_pair(t) for t in terms]):
            blocks += [jnp.where(hi_mask, t, 0.0).astype(BF16) for t in values]
        both = lax.dot_general(
            jnp.concatenate(blocks, axis=0),
            hot,
            (((1,), (1,)), ((), ())),
            preferred_element_type=F32,
        )
        local = local + (both[: 9 * n_hi] + both[9 * n_hi :])
    for k in range(9):
        for half in range(WIDE // LANES):
            piece = local[k * n_hi : (k + 1) * n_hi, half * LANES : (half + 1) * LANES]
            if per_row == 2:
                stat_send[:, k, half, :] = piece
            else:
                for h in range(n_hi):
                    stat_send[h * (WIDE // LANES) + half, k] = piece[h : h + 1]

    pl.semaphore_wait(barrier, n_dev - 1)

    def send_stats(r, sem):
        owner = wrap(own + r, n_own)
        target = owner * stride
        return pltpu.make_async_remote_copy(
            src_ref=stat_send.at[owner],
            dst_ref=stat_recv.at[wrap(img - target + n_img - 1, n_img)],
            send_sem=sem,
            recv_sem=stat_recv_sem,
            device_id=(target, lm),
            device_id_type=MESH,
        )

    repeat(1, n_own, lambda r: send_stats(r, stat_send_sem).start())

    def step_copy(r):
        block = table.at[pl.ds(own * per_row, per_row)]
        return pltpu.make_async_remote_copy(
            src_ref=block,
            dst_ref=block,
            send_sem=step_send_sem,
            recv_sem=step_recv_sem,
            device_id=(wrap(img + r, n_img), lm),
            device_id_type=MESH,
        )

    def wait_for(ref, sem):
        pltpu.make_async_copy(ref, ref, sem).wait()

    def own_part():
        wait_for(stat_recv, stat_recv_sem)
        total = stat_send[own] + jnp.sum(stat_recv[...], axis=0)
        steps = solve_points([total[k] for k in range(9)], damping_ref[0])
        for half in range(per_row):
            for a in range(3):
                table[own * per_row + half, a : a + 1] = steps[a][half : half + 1]
            table[own * per_row + half, 3:4] = jnp.zeros((1, LANES), F32)
        repeat(1, n_img, lambda r: step_copy(r).start())

    copies[3].wait()
    copies[4].wait()
    eye = lax.broadcasted_iota(jnp.int32, (groups, groups), 0) == lax.broadcasted_iota(
        jnp.int32, (groups, groups), 1
    )
    slot_column = jnp.sum(
        jnp.where(eye, slot_ref[...].astype(F32), 0.0), axis=1, keepdims=True
    )
    group_iota = lax.broadcasted_iota(jnp.int32, (groups, n_obs), 0)
    slot_row[...] = jnp.sum(
        jnp.where(group_iota == cam_ref[...], slot_column, 0.0), axis=0, keepdims=True
    ).astype(jnp.int32)

    if stride == 1:
        own_part()
        wait_for(table.at[pl.ds(0, rows - per_row)], step_recv_sem)
    else:
        is_owner = lax.rem(img, stride) == 0

        @pl.when(is_owner)
        def _():
            own_part()
            wait_for(table.at[pl.ds(0, rows - per_row)], step_recv_sem)

        @pl.when(jnp.logical_not(is_owner))
        def _():
            send_stats(0, extra_sem).start()
            wait_for(table, step_recv_sem)

    grid = table[...].reshape(n_hi, WIDE // LANES, 4, LANES)
    picked = [
        jnp.concatenate([grid[:, half, a, :] for half in range(WIDE // LANES)], axis=1)
        for a in range(3)
    ]
    pieces = []
    for part in zip(*[split_pair(t) for t in picked]):
        pieces += [t.astype(BF16) for t in part]
    table_rows = jnp.concatenate(pieces, axis=0)
    copies[5].wait()
    partial = jnp.zeros((groups, CAMP), F32)
    group_iota = lax.broadcasted_iota(jnp.int32, (groups, CHUNK), 0)
    for part in parts:
        found = jnp.dot(table_rows, lo_hot[:, part], preferred_element_type=F32)
        hi_mask = lax.broadcasted_iota(jnp.int32, (n_hi, CHUNK), 0) == point_ref[:, part] // WIDE
        cu, cv = resid_ref[0:1, part], resid_ref[1:2, part]
        for a in range(3):
            pair = found[a * n_hi : (a + 1) * n_hi] + found[(3 + a) * n_hi : (4 + a) * n_hi]
            step = jnp.sum(jnp.where(hi_mask, pair, 0.0), axis=0, keepdims=True)
            cu = cu + jac_ref[a : a + 1, part] * step
            cv = cv + jac_ref[3 + a : 4 + a, part] * step
        member = group_iota == slot_row[:, part]
        weights = jnp.concatenate(
            [jnp.where(member, c, 0.0).astype(BF16) for c in (cu, cv)], axis=0
        )
        product = jnp.dot(weights, cam_vmem[part, :], preferred_element_type=F32)
        partial = partial + (product[:groups, :CAMP] + product[groups:, CAMP:])
    part_send[...] = partial.reshape(n_dev, gpd, CAMP)

    every_peer(
        lambda peer_img, peer_lm, r: pltpu.make_async_remote_copy(
            src_ref=part_send.at[peer_img * n_lm + peer_lm],
            dst_ref=part_recv.at[r],
            send_sem=part_send_sem,
            recv_sem=part_recv_sem,
            device_id=(peer_img, peer_lm),
            device_id_type=MESH,
        ).start()
    )

    for row in range(rows):
        step_ref[:, row * LANES : (row + 1) * LANES] = table[row, 0:3]
    step_out = pltpu.make_async_copy(step_ref, step_hbm, out_sems.at[0])
    step_out.start()

    wait_for(stat_send.at[pl.ds(0, n_own - 1)], stat_send_sem)
    if stride == 1:
        wait_for(table.at[pl.ds(0, rows - per_row)], step_send_sem)
    else:

        @pl.when(is_owner)
        def _():
            def one_step(r, carry):
                wait_for(table.at[pl.ds(0, per_row)], step_send_sem)
                return carry

            lax.fori_loop(1, n_img, one_step, 0)

        @pl.when(jnp.logical_not(is_owner))
        def _():
            wait_for(stat_send.at[0], extra_sem)

    wait_for(part_recv, part_recv_sem)
    grad_ref[...] = part_send[me] + jnp.sum(part_recv[...], axis=0)
    grad_out = pltpu.make_async_copy(grad_ref, grad_hbm, out_sems.at[1])
    grad_out.start()
    wait_for(part_send.at[pl.ds(0, n_dev - 1)], part_send_sem)
    step_out.wait()
    grad_out.wait()


def write_out(step_in, grad_in, step_hbm, grad_hbm, step_held, grad_held, sems):
    arrive = [
        pltpu.make_async_copy(grad_in, grad_held, sems.at[0]),
        pltpu.make_async_copy(step_in, step_held, sems.at[1]),
    ]
    leave = [
        pltpu.make_async_copy(grad_held, grad_hbm, sems.at[2]),
        pltpu.make_async_copy(step_held, step_hbm, sems.at[3]),
    ]
    for copy in arrive:
        copy.start()
    for first, second in zip(arrive, leave):
        first.wait()
        second.start()
    for copy in leave:
        copy.wait()


def solution(mesh):
    n_img, n_lm = mesh.shape["img"], mesh.shape["lm"]
    n_dev = n_img * n_lm
    points = LM_BLOCKS * BLOCK
    rows = points // LANES
    n_own = min(n_img, rows)
    per_row = rows // n_own

    def per_device(jac_point, jac_cam, resid, point_ids, cam_ids, owner_slot, damping):
        n_obs = cam_ids.shape[0]
        groups = owner_slot.shape[0]
        gpd = groups // n_dev
        hbm = pl.BlockSpec(memory_space=pltpu.HBM)
        shapes = (
            jax.ShapeDtypeStruct((3, points), F32),
            jax.ShapeDtypeStruct((gpd, CAMP), F32),
        )
        results = pl.pallas_call(
            functools.partial(kernel, n_img, n_lm, n_own, groups),
            out_shape=shapes,
            in_specs=[pl.BlockSpec(memory_space=pltpu.SMEM)]
            + [hbm] * 6,
            out_specs=(hbm, hbm),
            scratch_shapes=[
                pltpu.VMEM((3, points), F32),
                pltpu.VMEM((gpd, CAMP), F32),
                pltpu.VMEM(jac_point.shape, F32),
                pltpu.VMEM(resid.shape, F32),
                pltpu.VMEM((1, n_obs), jnp.int32),
                pltpu.VMEM((1, n_obs), jnp.int32),
                pltpu.VMEM((1, groups), jnp.int32),
                pltpu.VMEM((1, n_obs), jnp.int32),
                pltpu.VMEM((n_obs, 2 * CAMP), BF16),
                pltpu.VMEM((WIDE, n_obs), BF16),
                pltpu.VMEM((n_own, 9, per_row, LANES), F32),
                pltpu.VMEM((n_img - 1, 9, per_row, LANES), F32),
                pltpu.VMEM((rows, 4, LANES), F32),
                pltpu.VMEM((n_dev, gpd, CAMP), F32),
                pltpu.VMEM((n_dev - 1, gpd, CAMP), F32),
            ]
            + [pltpu.SemaphoreType.DMA((6,)), pltpu.SemaphoreType.DMA((2,))]
            + [pltpu.SemaphoreType.DMA] * 7,
            compiler_params=pltpu.CompilerParams(
                collective_id=0,
                has_side_effects=True,
                vmem_limit_bytes=VMEM_BYTES,
            ),
        )(
            damping,
            jac_point,
            resid,
            point_ids.reshape(1, n_obs),
            cam_ids.reshape(1, n_obs),
            owner_slot.reshape(1, groups),
            jac_cam,
        )
        return pl.pallas_call(
            write_out,
            out_shape=shapes,
            in_specs=[hbm, hbm],
            out_specs=(hbm, hbm),
            scratch_shapes=[
                pltpu.VMEM((3, points), F32),
                pltpu.VMEM((gpd, CAMP), F32),
                pltpu.SemaphoreType.DMA((4,)),
            ],
            compiler_params=pltpu.CompilerParams(vmem_limit_bytes=VMEM_BYTES),
        )(*results)

    placed = (
        P(None, ("img", "lm")),
        P(("img", "lm"), None),
        P(None, ("img", "lm")),
        P(("img", "lm")),
        P(("img", "lm")),
        P(),
        P(),
    )
    return jax.shard_map(
        per_device,
        mesh=mesh,
        in_specs=placed,
        out_specs=(P(None, "lm"), P(("img", "lm"), None)),
        check_vma=False,
    )
```

```python
import functools
import jax
import jax.numpy as jnp
from jax import lax
from jax.experimental import pallas as pl
from jax.experimental.pallas import tpu as pltpu
from jax.sharding import PartitionSpec as P

CAMP = 128
BLOCK = 64
LM_BLOCKS = 64
LANES = 128
VMEM_BYTES = 2**26 - 2**18
WIDE = 256
MESH = pl.DeviceIdType.MESH
F32 = jnp.float32
BF16 = jnp.bfloat16


def split_pair(x):
    high = x.astype(BF16).astype(F32)
    low = (x - high).astype(BF16).astype(F32)
    return high, low


def solve_points(stats, factor):
    h01, h02, h12 = (stats[1], stats[2], stats[4])
    a00 = stats[0] + factor * (stats[0] + 1.0)
    a11 = stats[3] + factor * (stats[3] + 1.0)
    a22 = stats[5] + factor * (stats[5] + 1.0)
    g0, g1, g2 = (stats[6], stats[7], stats[8])
    c00 = a11 * a22 - h12 * h12
    c01 = h02 * h12 - h01 * a22
    c02 = h01 * h12 - h02 * a11
    c11 = a00 * a22 - h02 * h02
    c12 = h01 * h02 - a00 * h12
    c22 = a00 * a11 - h01 * h01
    determ = a00 * c00 + h01 * c01 + h02 * c02
    s0 = -(c00 * g0 + c01 * g1 + c02 * g2) / determ
    s1 = -(c01 * g0 + c11 * g1 + c12 * g2) / determ
    s2 = -(c02 * g0 + c12 * g1 + c22 * g2) / determ
    return s0, s1, s2


def kernel(
    n_img, n_lm, n_own, groups,
    damping_ref, jac_hbm, resid_hbm, point_hbm, cam_hbm, slot_hbm, jac_cam_hbm,
    step_hbm, grad_hbm,
    step_ref, grad_ref, jac_ref, resid_ref, point_ref, cam_ref, slot_ref, cam_vmem, lo_hot, stat_send, stat_recv, table, part_send, part_recv,
    in_sems, out_sems, stat_send_sem, stat_recv_sem, extra_sem,
    step_send_sem, step_recv_sem, part_send_sem, part_recv_sem,
):
    n_dev = n_img * n_lm
    n_obs = point_ref.shape[1]
    rows = LM_BLOCKS * BLOCK // LANES
    n_hi = LM_BLOCKS * BLOCK // WIDE
    per_row = rows // n_own
    stride = n_img // n_own
    gpd = groups // n_dev
    img, lm = lax.axis_index("img"), lax.axis_index("lm")
    me = img * n_lm + lm
    own = img // stride if stride > 1 else img

    copies = [
        pltpu.make_async_copy(source, target, in_sems.at[i])
        for i, (source, target) in enumerate(
            [
                (point_hbm, point_ref),
                (jac_hbm, jac_ref),
                (resid_hbm, resid_ref),
                (cam_hbm, cam_ref),
                (slot_hbm, slot_ref),
                (jac_cam_hbm, cam_vmem),
            ]
        )
    ]
    for copy in copies:
        copy.start()

    def wrap(index, extent):
        return jnp.where(index >= extent, index - extent, index)

    def repeat(first, last, body):
        if last <= 64:
            for r in range(first, last):
                body(r)
        else:
            lax.fori_loop(first, last, lambda r, carry: (body(r), carry)[1], 0)

    def every_peer(body):
        for d_lm in range(n_lm):
            peer_lm = wrap(lm + d_lm, n_lm)

            def one(d_img, d_lm=d_lm, peer_lm=peer_lm):
                body(wrap(img + d_img, n_img), peer_lm, d_img * n_lm + d_lm - 1)

            repeat(1 if d_lm == 0 else 0, n_img, one)

    barrier = pltpu.get_barrier_semaphore()
    every_peer(
        lambda peer_img, peer_lm, r: pl.semaphore_signal(
            barrier, inc=1, device_id=(peer_img, peer_lm), device_id_type=MESH
        )
    )

    copies[0].wait()
    point = point_ref[...]
    hi = point // WIDE
    lo = point - hi * WIDE
    hi_mask = lax.broadcasted_iota(jnp.int32, (n_hi, n_obs), 0) == hi
    lo_hot[...] = jnp.where(
        lax.broadcasted_iota(jnp.int32, (WIDE, n_obs), 0) == lo, 1.0, 0.0
    ).astype(BF16)
    copies[1].wait()
    copies[2].wait()
    u = [jac_ref[a : a + 1, :] for a in range(3)]
    v = [jac_ref[3 + a : 4 + a, :] for a in range(3)]
    ru, rv = resid_ref[0:1, :], resid_ref[1:2, :]
    terms = [u[a] * u[b] + v[a] * v[b] for a, b in ((0, 0), (0, 1), (0, 2), (1, 1), (1, 2), (2, 2))]
    terms += [u[a] * ru + v[a] * rv for a in range(3)]
    blocks = []
    for part in zip(*[split_pair(t) for t in terms]):
        blocks += [jnp.where(hi_mask, t, 0.0).astype(BF16) for t in part]
    left = jnp.concatenate(blocks, axis=0)
    both = lax.dot_general(
        left, lo_hot[...], (((1,), (1,)), ((), ())), preferred_element_type=F32
    )
    local = both[: 9 * n_hi] + both[9 * n_hi :]
    for k in range(9):
        for half in range(WIDE // LANES):
            piece = local[k * n_hi : (k + 1) * n_hi, half * LANES : (half + 1) * LANES]
            if per_row == 2:
                stat_send[:, k, half, :] = piece
            else:
                for h in range(n_hi):
                    stat_send[h * (WIDE // LANES) + half, k] = piece[h : h + 1]

    pl.semaphore_wait(barrier, n_dev - 1)

    def send_stats(r, sem):
        owner = wrap(own + r, n_own)
        target = owner * stride
        return pltpu.make_async_remote_copy(
            src_ref=stat_send.at[owner],
            dst_ref=stat_recv.at[wrap(img - target + n_img - 1, n_img)],
            send_sem=sem,
            recv_sem=stat_recv_sem,
            device_id=(target, lm),
            device_id_type=MESH,
        )

    repeat(1, n_own, lambda r: send_stats(r, stat_send_sem).start())

    def step_copy(r):
        block = table.at[pl.ds(own * per_row, per_row)]
        return pltpu.make_async_remote_copy(
            src_ref=block,
            dst_ref=block,
            send_sem=step_send_sem,
            recv_sem=step_recv_sem,
            device_id=(wrap(img + r, n_img), lm),
            device_id_type=MESH,
        )

    def wait_for(ref, sem):
        pltpu.make_async_copy(ref, ref, sem).wait()

    def own_part():
        wait_for(stat_recv, stat_recv_sem)
        total = stat_send[own] + jnp.sum(stat_recv[...], axis=0)
        steps = solve_points([total[k] for k in range(9)], damping_ref[0])
        for half in range(per_row):
            for a in range(3):
                table[own * per_row + half, a : a + 1] = steps[a][half : half + 1]
            table[own * per_row + half, 3:4] = jnp.zeros((1, LANES), F32)
        repeat(1, n_img, lambda r: step_copy(r).start())

    copies[3].wait()
    copies[4].wait()
    row_slot = slot_ref[...]
    eye = lax.broadcasted_iota(jnp.int32, (groups, groups), 0) == lax.broadcasted_iota(
        jnp.int32, (groups, groups), 1
    )
    slot_column = jnp.sum(
        jnp.where(eye, row_slot.astype(F32), 0.0), axis=1, keepdims=True
    )
    group_iota = lax.broadcasted_iota(jnp.int32, (groups, n_obs), 0)
    slots = jnp.sum(
        jnp.where(group_iota == cam_ref[...], slot_column, 0.0), axis=0, keepdims=True
    ).astype(jnp.int32)

    if stride == 1:
        own_part()
        wait_for(table.at[pl.ds(0, rows - per_row)], step_recv_sem)
    else:
        is_owner = lax.rem(img, stride) == 0

        @pl.when(is_owner)
        def _():
            own_part()
            wait_for(table.at[pl.ds(0, rows - per_row)], step_recv_sem)

        @pl.when(jnp.logical_not(is_owner))
        def _():
            send_stats(0, extra_sem).start()
            wait_for(table, step_recv_sem)

    grid = table[...].reshape(n_hi, WIDE // LANES, 4, LANES)
    picked = [
        jnp.concatenate([grid[:, half, a, :] for half in range(WIDE // LANES)], axis=1)
        for a in range(3)
    ]
    pieces = []
    for part in zip(*[split_pair(t) for t in picked]):
        pieces += [t.astype(BF16) for t in part]
    found = jnp.dot(jnp.concatenate(pieces, axis=0), lo_hot[...], preferred_element_type=F32)
    step_obs = []
    for a in range(3):
        both_parts = found[a * n_hi : (a + 1) * n_hi] + found[(3 + a) * n_hi : (4 + a) * n_hi]
        step_obs.append(jnp.sum(jnp.where(hi_mask, both_parts, 0.0), axis=0, keepdims=True))
    cu = ru + u[0] * step_obs[0] + u[1] * step_obs[1] + u[2] * step_obs[2]
    cv = rv + v[0] * step_obs[0] + v[1] * step_obs[1] + v[2] * step_obs[2]
    member = group_iota == slots
    weights = jnp.concatenate(
        [jnp.where(member, cu, 0.0).astype(BF16), jnp.where(member, cv, 0.0).astype(BF16)], axis=0
    )
    copies[5].wait()
    product = jnp.dot(weights, cam_vmem[...], preferred_element_type=F32)
    partial = product[:groups, :CAMP] + product[groups:, CAMP:]
    part_send[...] = partial.reshape(n_dev, gpd, CAMP)

    every_peer(
        lambda peer_img, peer_lm, r: pltpu.make_async_remote_copy(
            src_ref=part_send.at[peer_img * n_lm + peer_lm],
            dst_ref=part_recv.at[r],
            send_sem=part_send_sem,
            recv_sem=part_recv_sem,
            device_id=(peer_img, peer_lm),
            device_id_type=MESH,
        ).start()
    )

    for row in range(rows):
        step_ref[:, row * LANES : (row + 1) * LANES] = table[row, 0:3]
    step_out = pltpu.make_async_copy(step_ref, step_hbm, out_sems.at[0])
    step_out.start()

    wait_for(stat_send.at[pl.ds(0, n_own - 1)], stat_send_sem)
    if stride == 1:
        wait_for(table.at[pl.ds(0, rows - per_row)], step_send_sem)
    else:

        @pl.when(is_owner)
        def _():
            def one_step(r, carry):
                wait_for(table.at[pl.ds(0, per_row)], step_send_sem)
                return carry

            lax.fori_loop(1, n_img, one_step, 0)

        @pl.when(jnp.logical_not(is_owner))
        def _():
            wait_for(stat_send.at[0], extra_sem)

    wait_for(part_recv, part_recv_sem)
    grad_ref[...] = part_send[me] + jnp.sum(part_recv[...], axis=0)
    grad_out = pltpu.make_async_copy(grad_ref, grad_hbm, out_sems.at[1])
    grad_out.start()
    wait_for(part_send.at[pl.ds(0, n_dev - 1)], part_send_sem)
    step_out.wait()
    grad_out.wait()


def write_out(step_in, grad_in, step_hbm, grad_hbm, step_held, grad_held, sems):
    arrive = [
        pltpu.make_async_copy(grad_in, grad_held, sems.at[0]),
        pltpu.make_async_copy(step_in, step_held, sems.at[1]),
    ]
    leave = [
        pltpu.make_async_copy(grad_held, grad_hbm, sems.at[2]),
        pltpu.make_async_copy(step_held, step_hbm, sems.at[3]),
    ]
    for copy in arrive:
        copy.start()
    for first, second in zip(arrive, leave):
        first.wait()
        second.start()
    for copy in leave:
        copy.wait()


def solution(mesh):
    n_img, n_lm = mesh.shape["img"], mesh.shape["lm"]
    n_dev = n_img * n_lm
    points = LM_BLOCKS * BLOCK
    rows = points // LANES
    n_own = min(n_img, rows)
    per_row = rows // n_own

    def per_device(jac_point, jac_cam, resid, point_ids, cam_ids, owner_slot, damping):
        n_obs = cam_ids.shape[0]
        groups = owner_slot.shape[0]
        gpd = groups // n_dev
        hbm = pl.BlockSpec(memory_space=pltpu.HBM)
        shapes = (
            jax.ShapeDtypeStruct((3, points), F32),
            jax.ShapeDtypeStruct((gpd, CAMP), F32),
        )
        results = pl.pallas_call(
            functools.partial(kernel, n_img, n_lm, n_own, groups),
            out_shape=shapes,
            in_specs=[pl.BlockSpec(memory_space=pltpu.SMEM)]
            + [hbm] * 6,
            out_specs=(hbm, hbm),
            scratch_shapes=[
                pltpu.VMEM((3, points), F32),
                pltpu.VMEM((gpd, CAMP), F32),
                pltpu.VMEM(jac_point.shape, F32),
                pltpu.VMEM(resid.shape, F32),
                pltpu.VMEM((1, n_obs), jnp.int32),
                pltpu.VMEM((1, n_obs), jnp.int32),
                pltpu.VMEM((1, groups), jnp.int32),
                pltpu.VMEM((n_obs, 2 * CAMP), BF16),
                pltpu.VMEM((WIDE, n_obs), BF16),
                pltpu.VMEM((n_own, 9, per_row, LANES), F32),
                pltpu.VMEM((n_img - 1, 9, per_row, LANES), F32),
                pltpu.VMEM((rows, 4, LANES), F32),
                pltpu.VMEM((n_dev, gpd, CAMP), F32),
                pltpu.VMEM((n_dev - 1, gpd, CAMP), F32),
            ]
            + [pltpu.SemaphoreType.DMA((6,)), pltpu.SemaphoreType.DMA((2,))]
            + [pltpu.SemaphoreType.DMA] * 7,
            compiler_params=pltpu.CompilerParams(
                collective_id=0,
                has_side_effects=True,
                vmem_limit_bytes=VMEM_BYTES,
            ),
        )(
            damping,
            jac_point,
            resid,
            point_ids.reshape(1, n_obs),
            cam_ids.reshape(1, n_obs),
            owner_slot.reshape(1, groups),
            jac_cam,
        )
        return pl.pallas_call(
            write_out,
            out_shape=shapes,
            in_specs=[hbm, hbm],
            out_specs=(hbm, hbm),
            scratch_shapes=[
                pltpu.VMEM((3, points), F32),
                pltpu.VMEM((gpd, CAMP), F32),
                pltpu.SemaphoreType.DMA((4,)),
            ],
            compiler_params=pltpu.CompilerParams(vmem_limit_bytes=VMEM_BYTES),
        )(*results)

    placed = (
        P(None, ("img", "lm")),
        P(("img", "lm"), None),
        P(None, ("img", "lm")),
        P(("img", "lm")),
        P(("img", "lm")),
        P(),
        P(),
    )
    return jax.shard_map(
        per_device,
        mesh=mesh,
        in_specs=placed,
        out_specs=(P(None, "lm"), P(("img", "lm"), None)),
        check_vma=False,
    )
```

```python
import functools
import jax
import jax.numpy as jnp
from jax import lax
from jax.experimental import pallas as pl
from jax.experimental.pallas import tpu as pltpu
from jax.sharding import PartitionSpec as P

CAMP = 128
BLOCK = 64
LM_BLOCKS = 64
LANES = 128
VMEM_BYTES = 2**26 - 2**18
WIDE = 256
MESH = pl.DeviceIdType.MESH
F32 = jnp.float32
BF16 = jnp.bfloat16


def split_pair(x):
    high = x.astype(BF16).astype(F32)
    low = (x - high).astype(BF16).astype(F32)
    return high, low


def solve_points(stats, factor):
    h01, h02, h12 = (stats[1], stats[2], stats[4])
    a00 = stats[0] + factor * (stats[0] + 1.0)
    a11 = stats[3] + factor * (stats[3] + 1.0)
    a22 = stats[5] + factor * (stats[5] + 1.0)
    g0, g1, g2 = (stats[6], stats[7], stats[8])
    c00 = a11 * a22 - h12 * h12
    c01 = h02 * h12 - h01 * a22
    c02 = h01 * h12 - h02 * a11
    c11 = a00 * a22 - h02 * h02
    c12 = h01 * h02 - a00 * h12
    c22 = a00 * a11 - h01 * h01
    determ = a00 * c00 + h01 * c01 + h02 * c02
    s0 = -(c00 * g0 + c01 * g1 + c02 * g2) / determ
    s1 = -(c01 * g0 + c11 * g1 + c12 * g2) / determ
    s2 = -(c02 * g0 + c12 * g1 + c22 * g2) / determ
    return s0, s1, s2


def kernel(
    n_img, n_lm, n_own, groups,
    damping_ref, jac_hbm, resid_hbm, point_hbm, cam_hbm, slot_hbm, jac_cam_hbm,
    step_hbm, grad_hbm,
    step_ref, grad_ref, jac_ref, resid_ref, point_ref, cam_ref, slot_ref, cam_vmem, lo_hot, stat_send, stat_recv, table, part_send, part_recv,
    in_sems, out_sems, stat_send_sem, stat_recv_sem, extra_sem,
    step_send_sem, step_recv_sem, part_send_sem, part_recv_sem,
):
    n_dev = n_img * n_lm
    n_obs = point_ref.shape[1]
    rows = LM_BLOCKS * BLOCK // LANES
    n_hi = LM_BLOCKS * BLOCK // WIDE
    per_row = rows // n_own
    stride = n_img // n_own
    gpd = groups // n_dev
    img, lm = lax.axis_index("img"), lax.axis_index("lm")
    me = img * n_lm + lm
    own = img // stride if stride > 1 else img

    copies = [
        pltpu.make_async_copy(source, target, in_sems.at[i])
        for i, (source, target) in enumerate(
            [
                (point_hbm, point_ref),
                (jac_hbm, jac_ref),
                (resid_hbm, resid_ref),
                (cam_hbm, cam_ref),
                (slot_hbm, slot_ref),
                (jac_cam_hbm, cam_vmem),
            ]
        )
    ]
    for copy in copies:
        copy.start()

    def wrap(index, extent):
        return jnp.where(index >= extent, index - extent, index)

    def repeat(first, last, body):
        if last <= 64:
            for r in range(first, last):
                body(r)
        else:
            lax.fori_loop(first, last, lambda r, carry: (body(r), carry)[1], 0)

    def every_peer(body):
        for d_lm in range(n_lm):
            peer_lm = wrap(lm + d_lm, n_lm)

            def one(d_img, d_lm=d_lm, peer_lm=peer_lm):
                body(wrap(img + d_img, n_img), peer_lm, d_img * n_lm + d_lm - 1)

            repeat(1 if d_lm == 0 else 0, n_img, one)

    barrier = pltpu.get_barrier_semaphore()
    every_peer(
        lambda peer_img, peer_lm, r: pl.semaphore_signal(
            barrier, inc=1, device_id=(peer_img, peer_lm), device_id_type=MESH
        )
    )

    copies[0].wait()
    point = point_ref[...]
    hi = lax.shift_right_logical(point, WIDE.bit_length() - 1)
    lo = lax.bitwise_and(point, WIDE - 1)
    hi_mask = lax.broadcasted_iota(jnp.int32, (n_hi, n_obs), 0) == hi
    lo_hot[...] = jnp.where(
        lax.broadcasted_iota(jnp.int32, (WIDE, n_obs), 0) == lo, 1.0, 0.0
    ).astype(BF16)
    copies[1].wait()
    copies[2].wait()
    u = [jac_ref[a : a + 1, :] for a in range(3)]
    v = [jac_ref[3 + a : 4 + a, :] for a in range(3)]
    ru, rv = resid_ref[0:1, :], resid_ref[1:2, :]
    terms = [u[a] * u[b] + v[a] * v[b] for a, b in ((0, 0), (0, 1), (0, 2), (1, 1), (1, 2), (2, 2))]
    terms += [u[a] * ru + v[a] * rv for a in range(3)]
    blocks = []
    for part in zip(*[split_pair(t) for t in terms]):
        blocks += [jnp.where(hi_mask, t, 0.0).astype(BF16) for t in part]
    left = jnp.concatenate(blocks, axis=0)
    both = lax.dot_general(
        left, lo_hot[...], (((1,), (1,)), ((), ())), preferred_element_type=F32
    )
    local = both[: 9 * n_hi] + both[9 * n_hi :]
    for k in range(9):
        for half in range(WIDE // LANES):
            piece = local[k * n_hi : (k + 1) * n_hi, half * LANES : (half + 1) * LANES]
            if per_row == 2:
                stat_send[:, k, half, :] = piece
            else:
                for h in range(n_hi):
                    stat_send[h * (WIDE // LANES) + half, k] = piece[h : h + 1]

    pl.semaphore_wait(barrier, n_dev - 1)

    def send_stats(r, sem):
        owner = wrap(own + r, n_own)
        target = owner * stride
        return pltpu.make_async_remote_copy(
            src_ref=stat_send.at[owner],
            dst_ref=stat_recv.at[wrap(img - target + n_img - 1, n_img)],
            send_sem=sem,
            recv_sem=stat_recv_sem,
            device_id=(target, lm),
            device_id_type=MESH,
        )

    repeat(1, n_own, lambda r: send_stats(r, stat_send_sem).start())

    def step_copy(r):
        block = table.at[pl.ds(own * per_row, per_row)]
        return pltpu.make_async_remote_copy(
            src_ref=block,
            dst_ref=block,
            send_sem=step_send_sem,
            recv_sem=step_recv_sem,
            device_id=(wrap(img + r, n_img), lm),
            device_id_type=MESH,
        )

    def wait_for(ref, sem):
        pltpu.make_async_copy(ref, ref, sem).wait()

    def own_part():
        wait_for(stat_recv, stat_recv_sem)
        total = stat_send[own] + jnp.sum(stat_recv[...], axis=0)
        steps = solve_points([total[k] for k in range(9)], damping_ref[0])
        for half in range(per_row):
            for a in range(3):
                table[own * per_row + half, a : a + 1] = steps[a][half : half + 1]
            table[own * per_row + half, 3:4] = jnp.zeros((1, LANES), F32)
        repeat(1, n_img, lambda r: step_copy(r).start())

    copies[3].wait()
    copies[4].wait()
    row_slot = slot_ref[...]
    eye = lax.broadcasted_iota(jnp.int32, (groups, groups), 0) == lax.broadcasted_iota(
        jnp.int32, (groups, groups), 1
    )
    slot_column = jnp.sum(
        jnp.where(eye, row_slot.astype(F32), 0.0), axis=1, keepdims=True
    )
    group_iota = lax.broadcasted_iota(jnp.int32, (groups, n_obs), 0)
    slots = jnp.sum(
        jnp.where(group_iota == cam_ref[...], slot_column, 0.0), axis=0, keepdims=True
    ).astype(jnp.int32)

    if stride == 1:
        own_part()
        wait_for(table.at[pl.ds(0, rows - per_row)], step_recv_sem)
    else:
        is_owner = lax.rem(img, stride) == 0

        @pl.when(is_owner)
        def _():
            own_part()
            wait_for(table.at[pl.ds(0, rows - per_row)], step_recv_sem)

        @pl.when(jnp.logical_not(is_owner))
        def _():
            send_stats(0, extra_sem).start()
            wait_for(table, step_recv_sem)

    grid = table[...].reshape(n_hi, WIDE // LANES, 4, LANES)
    picked = [
        jnp.concatenate([grid[:, half, a, :] for half in range(WIDE // LANES)], axis=1)
        for a in range(3)
    ]
    pieces = []
    for part in zip(*[split_pair(t) for t in picked]):
        pieces += [t.astype(BF16) for t in part]
    found = jnp.dot(jnp.concatenate(pieces, axis=0), lo_hot[...], preferred_element_type=F32)
    step_obs = []
    for a in range(3):
        both_parts = found[a * n_hi : (a + 1) * n_hi] + found[(3 + a) * n_hi : (4 + a) * n_hi]
        step_obs.append(jnp.sum(jnp.where(hi_mask, both_parts, 0.0), axis=0, keepdims=True))
    cu = ru + u[0] * step_obs[0] + u[1] * step_obs[1] + u[2] * step_obs[2]
    cv = rv + v[0] * step_obs[0] + v[1] * step_obs[1] + v[2] * step_obs[2]
    member = group_iota == slots
    weights = jnp.concatenate(
        [jnp.where(member, cu, 0.0).astype(BF16), jnp.where(member, cv, 0.0).astype(BF16)], axis=0
    )
    copies[5].wait()
    product = jnp.dot(weights, cam_vmem[...], preferred_element_type=F32)
    partial = product[:groups, :CAMP] + product[groups:, CAMP:]
    part_send[...] = partial.reshape(n_dev, gpd, CAMP)

    every_peer(
        lambda peer_img, peer_lm, r: pltpu.make_async_remote_copy(
            src_ref=part_send.at[peer_img * n_lm + peer_lm],
            dst_ref=part_recv.at[r],
            send_sem=part_send_sem,
            recv_sem=part_recv_sem,
            device_id=(peer_img, peer_lm),
            device_id_type=MESH,
        ).start()
    )

    for row in range(rows):
        step_ref[:, row * LANES : (row + 1) * LANES] = table[row, 0:3]
    step_out = pltpu.make_async_copy(step_ref, step_hbm, out_sems.at[0])
    step_out.start()

    wait_for(stat_send.at[pl.ds(0, n_own - 1)], stat_send_sem)
    if stride == 1:
        wait_for(table.at[pl.ds(0, rows - per_row)], step_send_sem)
    else:

        @pl.when(is_owner)
        def _():
            def one_step(r, carry):
                wait_for(table.at[pl.ds(0, per_row)], step_send_sem)
                return carry

            lax.fori_loop(1, n_img, one_step, 0)

        @pl.when(jnp.logical_not(is_owner))
        def _():
            wait_for(stat_send.at[0], extra_sem)

    wait_for(part_recv, part_recv_sem)
    grad_ref[...] = part_send[me] + jnp.sum(part_recv[...], axis=0)
    grad_out = pltpu.make_async_copy(grad_ref, grad_hbm, out_sems.at[1])
    grad_out.start()
    wait_for(part_send.at[pl.ds(0, n_dev - 1)], part_send_sem)
    step_out.wait()
    grad_out.wait()


def write_out(step_in, grad_in, step_hbm, grad_hbm, step_held, grad_held, sems):
    arrive = [
        pltpu.make_async_copy(grad_in, grad_held, sems.at[0]),
        pltpu.make_async_copy(step_in, step_held, sems.at[1]),
    ]
    leave = [
        pltpu.make_async_copy(grad_held, grad_hbm, sems.at[2]),
        pltpu.make_async_copy(step_held, step_hbm, sems.at[3]),
    ]
    for copy in arrive:
        copy.start()
    for first, second in zip(arrive, leave):
        first.wait()
        second.start()
    for copy in leave:
        copy.wait()


def solution(mesh):
    n_img, n_lm = mesh.shape["img"], mesh.shape["lm"]
    n_dev = n_img * n_lm
    points = LM_BLOCKS * BLOCK
    rows = points // LANES
    n_own = min(n_img, rows)
    per_row = rows // n_own

    def per_device(jac_point, jac_cam, resid, point_ids, cam_ids, owner_slot, damping):
        n_obs = cam_ids.shape[0]
        groups = owner_slot.shape[0]
        gpd = groups // n_dev
        hbm = pl.BlockSpec(memory_space=pltpu.HBM)
        shapes = (
            jax.ShapeDtypeStruct((3, points), F32),
            jax.ShapeDtypeStruct((gpd, CAMP), F32),
        )
        results = pl.pallas_call(
            functools.partial(kernel, n_img, n_lm, n_own, groups),
            out_shape=shapes,
            in_specs=[pl.BlockSpec(memory_space=pltpu.SMEM)]
            + [hbm] * 6,
            out_specs=(hbm, hbm),
            scratch_shapes=[
                pltpu.VMEM((3, points), F32),
                pltpu.VMEM((gpd, CAMP), F32),
                pltpu.VMEM(jac_point.shape, F32),
                pltpu.VMEM(resid.shape, F32),
                pltpu.VMEM((1, n_obs), jnp.int32),
                pltpu.VMEM((1, n_obs), jnp.int32),
                pltpu.VMEM((1, groups), jnp.int32),
                pltpu.VMEM((n_obs, 2 * CAMP), BF16),
                pltpu.VMEM((WIDE, n_obs), BF16),
                pltpu.VMEM((n_own, 9, per_row, LANES), F32),
                pltpu.VMEM((n_img - 1, 9, per_row, LANES), F32),
                pltpu.VMEM((rows, 4, LANES), F32),
                pltpu.VMEM((n_dev, gpd, CAMP), F32),
                pltpu.VMEM((n_dev - 1, gpd, CAMP), F32),
            ]
            + [pltpu.SemaphoreType.DMA((6,)), pltpu.SemaphoreType.DMA((2,))]
            + [pltpu.SemaphoreType.DMA] * 7,
            compiler_params=pltpu.CompilerParams(
                collective_id=0,
                has_side_effects=True,
                vmem_limit_bytes=VMEM_BYTES,
            ),
        )(
            damping,
            jac_point,
            resid,
            point_ids.reshape(1, n_obs),
            cam_ids.reshape(1, n_obs),
            owner_slot.reshape(1, groups),
            jac_cam,
        )
        return pl.pallas_call(
            write_out,
            out_shape=shapes,
            in_specs=[hbm, hbm],
            out_specs=(hbm, hbm),
            scratch_shapes=[
                pltpu.VMEM((3, points), F32),
                pltpu.VMEM((gpd, CAMP), F32),
                pltpu.SemaphoreType.DMA((4,)),
            ],
            compiler_params=pltpu.CompilerParams(vmem_limit_bytes=VMEM_BYTES),
        )(*results)

    placed = (
        P(None, ("img", "lm")),
        P(("img", "lm"), None),
        P(None, ("img", "lm")),
        P(("img", "lm")),
        P(("img", "lm")),
        P(),
        P(),
    )
    return jax.shard_map(
        per_device,
        mesh=mesh,
        in_specs=placed,
        out_specs=(P(None, "lm"), P(("img", "lm"), None)),
        check_vma=False,
    )
```
